1024 devices in a mesh: dp: 64 (over x, y_lo, core), mp: 16 (over z, y_hi).
Axes of the slice: x: 8, y: 8 (y_hi: 2, y_lo: 4; y = y_hi * 4 + y_lo), z: 8, core: 2. Of those that a mesh axis runs over, the one named last changes fastest.
Arguments:
- activations: bfloat16 [16384, 8192], P('dp', 'mp'), may hold values from -6 to 6
- out_grads: bfloat16 [16384, 14336], P('dp', 'mp'), may hold values from -0.046875 to 0.046875
- basis: bfloat16 [8192, 1024], P('mp'), may hold values from -0.0625 to 0.0625
- first_moment: float32 [1024, 14336], P('dp', 'mp'), may hold values from -3 to 3
- second_moment: float32 [1024, 14336], P('dp', 'mp'), may hold values from 0.05 to 2
Outputs:
- weight_step: float32 [8192, 14336], P('dp', 'mp')
- new_first: float32 [1024, 14336], P('dp', 'mp')
- new_second: float32 [1024, 14336], P('dp', 'mp')
The draws below stay inside these ranges and needn't reach their ends.
All inputs are finite; a program needn't handle non-finite values.
Results may differ from the reference program's by a relative error of at most 0.0031.
Values may be sent and summed in bfloat16 or wider, within the bound.
A program may use at most 32 MiB of HBM per device.

```python
import math
import jax
import jax.numpy as jnp
from jax import lax

D = 8192
RANK = 1024
STEP = 10
FF = 14336
TOKENS = 16384


def block_scale(own_key, extent, cuts, smallest, high):
    def one(dim, parts):
        draws = jax.random.uniform(jax.random.fold_in(jax.random.fold_in(own_key, 6), dim), (parts,), jnp.float32, smallest / len(cuts), high / len(cuts))
        return jnp.repeat(jnp.exp(draws), extent[dim] // parts).reshape((-1,) + (1,) * (len(extent) - dim - 1))

    gain = one(*cuts[0])
    for cut in cuts[1:]:
        gain = gain * one(*cut)
    return gain


def centred(stream_key, extent, scale, limit, shards=(), dtype=jnp.bfloat16):
    values = scale * jax.random.normal(stream_key, extent, jnp.float32)
    if shards:
        values = values * block_scale(stream_key, extent, shards, -0.22, 0.18)
    return jnp.clip(values, -limit, limit).astype(dtype)


def setup_inputs(seed: int = 0) -> dict:
    seeds = jax.random.split(jax.random.key(seed), 6)
    activations = centred(seeds[0], (TOKENS, D), 1.0, 6.0, ((0, 64), (1, 16)))
    out_grads = centred(seeds[1], (TOKENS, FF), TOKENS ** -0.5, 0.046875, ((0, 64), (1, 16)))
    basis = centred(seeds[2], (D, RANK), D ** -0.5, 0.0625, ((0, 16),))
    first_moment = centred(seeds[3], (RANK, FF), 0.3, 3.0, ((0, 64), (1, 16)), jnp.float32)
    second_moment = jnp.clip(jnp.exp(math.log(2.0) - 3.6888794 * jax.random.uniform(seeds[4], (RANK, FF), jnp.float32) ** block_scale(seeds[4], (RANK, FF), ((0, 64), (1, 16)), -0.2, 0.2)), 0.05, 2.0)
    return {"activations": activations, "out_grads": out_grads, "basis": basis, "first_moment": first_moment, "second_moment": second_moment}


beta_first = 0.9
beta_second = 0.95
adam_eps = 1e-08
galore_scale = 0.25

def reference(activations, out_grads, basis, first_moment, second_moment):
    projected = jnp.dot(activations, basis, preferred_element_type=jnp.float32).astype(jnp.bfloat16)
    gradient = lax.dot_general(projected, out_grads, (((0,), (0,)), ((), ())), preferred_element_type=jnp.float32)
    new_first = beta_first * first_moment + (1.0 - beta_first) * gradient
    new_second = beta_second * second_moment + (1.0 - beta_second) * gradient * gradient
    first_hat = new_first / (1.0 - beta_first ** STEP)
    second_hat = new_second / (1.0 - beta_second ** STEP)
    direction = (first_hat / (jnp.sqrt(second_hat) + adam_eps)).astype(jnp.bfloat16)
    weight_step = galore_scale * jnp.dot(basis, direction, preferred_element_type=jnp.float32)
    return (weight_step, new_first, new_second)
```

```python
import jax
import jax.numpy as jnp
from jax import lax
from jax.experimental import pallas as pl
from jax.experimental.pallas import tpu as pltpu
from jax.sharding import PartitionSpec as P

STEP = 10

beta_first = 0.9
beta_second = 0.95
adam_eps = 1e-08
galore_scale = 0.25

NX, NY, NZ = 8, 4, 8
RANK = 1024
TOK = 256
FF = 896
CHUNK = RANK // NX
ROWS = 16
XF = 512
YF = FF - XF
OFFSETS = (4, 3, 5, 2, 6, 1, 7)
NEAR = (1, 7, 2, 6, 3, 5, 4)

f32, bf16 = jnp.float32, jnp.bfloat16

names = (
    ("reduce_z", NZ), ("pair_h", 1), ("gather_z", NZ), ("pair_core", NX), ("first_x", NX), ("first_y", NY * NX),
    ("second_y", NY), ("second_x", NX), ("dir_x", NX), ("dir_y", NY), ("all_y", NY), ("all_x", NX),
    ("core_one", NY), ("core_two", NX), ("rows_h", 1), ("rows_z", NZ),
)
BASE, SEMS = {}, 0
for name, count in names:
    BASE[name] = SEMS
    SEMS += count


def kernel(
    act, grads, basis, first, second, step_out, first_out, second_out,
    part_send, part_recv, half, half_recv, turned, turned_recv, full, core_recv, mine, x_send, x_recv,
    y_send, y_recv, t_send, t_recv, u_send, u_recv, dir_one, dir_two, rows, send, recv,
):
    dp, mp = lax.axis_index("dp"), lax.axis_index("mp")
    x, y, c = dp // (2 * NY), dp // 2 % NY, dp % 2
    z, h = mp // 2, mp % 2

    def at_x(k):
        return (((x + k) % NX * NY + y) * 2 + c, mp)

    def at_y(k):
        return ((x * NY + (y + k) % NY) * 2 + c, mp)

    def at_z(k):
        return (dp, (z + k) % NZ * 2 + h)

    at_h = (dp, z * 2 + 1 - h)
    at_core = (dp + 1 - 2 * c, mp)

    def move(source, target, name, place, device, recv_place=None):
        recv_place = place if recv_place is None else recv_place
        return pltpu.make_async_remote_copy(
            src_ref=source, dst_ref=target, send_sem=send.at[BASE[name] + place],
            recv_sem=recv.at[BASE[name] + recv_place], device_id=device, device_id_type=pl.DeviceIdType.MESH,
        )

    barrier = pltpu.get_barrier_semaphore()
    partners = [at_x(k) for k in range(1, NX)] + [at_y(k) for k in range(1, NY)] + [at_z(k) for k in range(1, NZ)]
    partners += [at_h, at_core]
    for device in partners:
        pl.semaphore_signal(barrier, inc=1, device_id=device, device_id_type=pl.DeviceIdType.MESH)

    holds = z == x
    owns = jnp.logical_and(holds, h == y // 2)

    @pl.when(owns)
    def _():
        rows[...] = basis[pl.ds(pl.multiple_of((y % 2 * 2 + c) * 128, 128), 128), :]

    def rows_h():
        return move(rows, rows, "rows_h", 0, at_h)

    def rows_z(k):
        return move(rows, rows, "rows_z", k, at_z(k), 0)

    def columns(k):
        return pl.ds(pl.multiple_of((z + k + x) % NX * CHUNK, CHUNK), CHUNK)

    def project(k):
        return jnp.dot(act[...], basis[:, columns(k)], preferred_element_type=f32)

    part_send[OFFSETS[0]] = project(OFFSETS[0]).astype(bf16)
    pl.semaphore_wait(barrier, len(partners))
    copies = []
    for k in OFFSETS:
        if k != OFFSETS[0]:
            part_send[k] = project(k).astype(bf16)
        copy = move(part_send.at[k], part_recv.at[k], "reduce_z", k, at_z(k))
        copy.start()
        copies.append(copy)

    @pl.when(owns)
    def _():
        rows_h().start()

    total = project(0)
    for copy, k in zip(copies, OFFSETS):
        copy.wait()
    for k in range(1, NZ):
        total = total + part_recv[k].astype(f32)
    half[...] = total
    copy = move(half, half_recv, "pair_h", 0, at_h)
    copy.start()
    copy.wait()
    turned[...] = jnp.transpose(half[...] + half_recv[...]).astype(bf16)

    gathers = {}
    for k in OFFSETS:
        gathers[k] = move(turned, turned_recv.at[k], "gather_z", k, at_z(k))
        gathers[k].start()

    def away(k):
        return (z - k + NZ) % NX

    def to_core(k):
        return move(full.at[k, :, 1 - c], core_recv.at[k], "pair_core", k, at_core)

    def to_x(o):
        return move(x_send.at[o], x_recv.at[o], "first_x", o, at_x(o))

    def to_y(q, o):
        return move(y_send.at[o, (y + q) % NY], y_recv.at[q, o], "first_y", q * NX + o, at_y(q))

    def sum_cores(k):
        to_core(k).wait_recv()
        o = away(k)
        both = full[k, :, c] + core_recv[k]
        mine[o] = both
        x_send[o] = both[:, :, :XF].astype(bf16)
        y_send[o] = both[:, :, XF:].astype(bf16)

        @pl.when(o != 0)
        def _():
            to_x(o).start()

        for q in range(1, NY):
            to_y(q, o).start()

    order = (0,) + NEAR
    for place, k in enumerate(order):
        if k:
            gathers[k].wait_recv()
            block = turned_recv[k]
        else:
            block = turned[...]
        product = jnp.dot(block, grads[...], preferred_element_type=f32)
        full[k] = product.reshape(NY, 2, ROWS, FF)
        to_core(k).start()
        if place:
            sum_cores(order[place - 1])
    sum_cores(order[-1])

    @pl.when(jnp.logical_and(holds, jnp.logical_not(owns)))
    def _():
        rows_h().wait_recv()

    @pl.when(holds)
    def _():
        for k in OFFSETS:
            rows_z(k).start()

    second_x, second_y = [], []
    for o in range(NX):
        for q in range(1, NY):
            to_y(q, o).wait_recv()
        value = mine[o, y][:, XF:]
        for q in range(1, NY):
            value = value + y_recv[q, o].astype(f32)
        u_send[o] = value
        if o:
            copy = move(u_send.at[o], u_recv.at[o], "second_x", o, at_x(o))
            copy.start()
            second_x.append(copy)
    for o in range(1, NX):
        to_x(o).wait_recv()
    value = mine[0][:, :, :XF]
    for o in range(1, NX):
        value = value + x_recv[o].astype(f32)
    t_send[...] = value
    for q in range(1, NY):
        copy = move(t_send.at[(y + q) % NY], t_recv.at[q], "second_y", q, at_y(q))
        copy.start()
        second_y.append(copy)

    def adam(gradient, columns, target):
        new_first = beta_first * first[:, columns] + (1.0 - beta_first) * gradient
        new_second = beta_second * second[:, columns] + (1.0 - beta_second) * gradient * gradient
        first_hat = new_first / (1.0 - beta_first**STEP)
        second_hat = new_second / (1.0 - beta_second**STEP)
        first_out[:, columns] = new_first
        second_out[:, columns] = new_second
        target[x, y, c] = (first_hat / (jnp.sqrt(second_hat) + adam_eps)).astype(bf16)

    dir_x, dir_y, all_x, all_y, core_one, core_two = [], [], [], [], [], []
    for copy in second_x:
        copy.wait_recv()
    value = u_send[0]
    for o in range(1, NX):
        value = value + u_recv[o]
    adam(value, slice(XF, FF), dir_two)
    for q in range(1, NY):
        copy = move(dir_two.at[x, y, c], dir_two.at[x, y, c], "dir_y", q, at_y(q))
        copy.start()
        dir_y.append(copy)
    for copy in second_y:
        copy.wait_recv()
    value = t_send[y]
    for q in range(1, NY):
        value = value + t_recv[q]
    adam(value, slice(0, XF), dir_one)
    for o in OFFSETS:
        copy = move(dir_one.at[x, y, c], dir_one.at[x, y, c], "dir_x", o, at_x(o))
        copy.start()
        dir_x.append(copy)

    def core_rows_one(q):
        block = dir_one.at[:, (y + NY - q) % NY, c]
        return move(block, block, "core_one", q, at_core)

    def core_rows_two(o):
        block = dir_two.at[(x + NX - o) % NX, :, c]
        return move(block, block, "core_two", o, at_core)

    for copy in dir_y:
        copy.wait_recv()
    for o in OFFSETS:
        copy = move(dir_two.at[x, :, c], dir_two.at[x, :, c], "all_x", o, at_x(o))
        copy.start()
        all_x.append(copy)
    core_two.append(core_rows_two(0))
    core_two[-1].start()
    for copy in dir_x:
        copy.wait_recv()
    for q in range(1, NY):
        copy = move(dir_one.at[:, y, c], dir_one.at[:, y, c], "all_y", q, at_y(q))
        copy.start()
        all_y.append(copy)
    core_one.append(core_rows_one(0))
    core_one[-1].start()
    by_offset = dict(zip(OFFSETS, all_x))
    for o in NEAR:
        by_offset[o].wait_recv()
        core_two.append(core_rows_two(o))
        core_two[-1].start()
    for q in (1, 3, 2):
        all_y[q - 1].wait_recv()
        core_one.append(core_rows_one(q))
        core_one[-1].start()

    @pl.when(jnp.logical_not(holds))
    def _():
        rows_z(0).wait_recv()

    for copy in core_two:
        copy.wait_recv()
    step_out[:, XF:] = galore_scale * jnp.dot(
        rows[...], dir_two[...].reshape(RANK, YF), preferred_element_type=f32
    )
    for copy in core_one:
        copy.wait_recv()
    step_out[:, :XF] = galore_scale * jnp.dot(
        rows[...], dir_one[...].reshape(RANK, XF), preferred_element_type=f32
    )

    for k in OFFSETS:
        gathers[k].wait_send()
    for k in range(NX):
        to_core(k).wait_send()
    for o in range(NX):
        if o:
            to_x(o).wait_send()
        for q in range(1, NY):
            to_y(q, o).wait_send()
    for copy in second_x + second_y + dir_x + dir_y + all_x + all_y + core_one + core_two:
        copy.wait_send()

    @pl.when(owns)
    def _():
        rows_h().wait_send()

    @pl.when(holds)
    def _():
        for k in OFFSETS:
            rows_z(k).wait_send()


def body(activations, out_grads, basis, first_moment, second_moment):
    vmem = pl.BlockSpec(memory_space=pltpu.VMEM)
    return pl.pallas_call(
        kernel,
        out_shape=(
            jax.ShapeDtypeStruct((128, FF), f32),
            jax.ShapeDtypeStruct((ROWS, FF), f32),
            jax.ShapeDtypeStruct((ROWS, FF), f32),
        ),
        in_specs=[vmem] * 5,
        out_specs=(vmem,) * 3,
        scratch_shapes=[
            pltpu.VMEM((NZ, TOK, CHUNK), bf16),
            pltpu.VMEM((NZ, TOK, CHUNK), bf16),
            pltpu.VMEM((TOK, CHUNK), f32),
            pltpu.VMEM((TOK, CHUNK), f32),
            pltpu.VMEM((CHUNK, TOK), bf16),
            pltpu.VMEM((NZ, CHUNK, TOK), bf16),
            pltpu.VMEM((NX, NY, 2, ROWS, FF), f32),
            pltpu.VMEM((NX, NY, ROWS, FF), f32),
            pltpu.VMEM((NX, NY, ROWS, FF), f32),
            pltpu.VMEM((NX, NY, ROWS, XF), bf16),
            pltpu.VMEM((NX, NY, ROWS, XF), bf16),
            pltpu.VMEM((NX, NY, ROWS, YF), bf16),
            pltpu.VMEM((NY, NX, ROWS, YF), bf16),
            pltpu.VMEM((NY, ROWS, XF), f32),
            pltpu.VMEM((NY, ROWS, XF), f32),
            pltpu.VMEM((NX, ROWS, YF), f32),
            pltpu.VMEM((NX, ROWS, YF), f32),
            pltpu.VMEM((NX, NY, 2, ROWS, XF), bf16),
            pltpu.VMEM((NX, NY, 2, ROWS, YF), bf16),
            pltpu.VMEM((128, RANK), bf16),
            pltpu.SemaphoreType.DMA((SEMS,)),
            pltpu.SemaphoreType.DMA((SEMS,)),
        ],
        compiler_params=pltpu.CompilerParams(
            collective_id=0, has_side_effects=True, vmem_limit_bytes=40 << 20
        ),
        cost_estimate=pl.CostEstimate(flops=10**9, bytes_accessed=4 << 20, transcendentals=0),
        name="galore_step",
    )(activations, out_grads, basis, first_moment, second_moment)


def solution(mesh):
    return jax.shard_map(
        body,
        mesh=mesh,
        in_specs=(P("dp", "mp"), P("dp", "mp"), P("mp", None), P("dp", "mp"), P("dp", "mp")),
        out_specs=(P("dp", "mp"), P("dp", "mp"), P("dp", "mp")),
        check_vma=False,
    )
```

```python
import jax
import jax.numpy as jnp
from jax import lax
from jax.experimental import pallas as pl
from jax.experimental.pallas import tpu as pltpu
from jax.sharding import PartitionSpec as P

STEP = 10

beta_first = 0.9
beta_second = 0.95
adam_eps = 1e-08
galore_scale = 0.25

NX, NY, NZ = 8, 4, 8
RANK = 1024
TOK = 256
FF = 896
CHUNK = RANK // NX
PARTS = 2
PART = CHUNK // PARTS
PART_Y = NY // PARTS
BEHIND = 3
ROWS = 16
XF = 384
YF = FF - XF
OFFSETS = (4, 3, 5, 2, 6, 1, 7)
NEAR = (1, 7, 2, 6, 3, 5, 4)
SIDES = (1, 3, 2)

f32, bf16 = jnp.float32, jnp.bfloat16

names = (
    ("reduce_z", PARTS * NZ), ("pair_h", PARTS), ("gather_z", PARTS * NZ), ("pair_core", PARTS * NX),
    ("first_x", PARTS * NX), ("first_y", NY * NX),
    ("second_y", NY), ("second_x", NX), ("one", NY * NX), ("two", NY * NX), ("core_one", NY * NX),
    ("core_two", NY * NX), ("rows_h", 1), ("rows_z", NZ),
)
BASE, SEMS = {}, 0
for name, count in names:
    BASE[name] = SEMS
    SEMS += count


def kernel(
    act_in, grads_in, basis_in, first_in, second_in, step_out, first_out, second_out,
    act, grads, basis, first, second,
    own, part_send, part_recv, half, half_recv, turned, turned_recv, full, core_recv, mine, x_send, x_recv,
    y_send, y_recv, t_send, t_recv, u_send, u_recv, dir_one, dir_two, rows, send, recv, load,
):
    dp, mp = lax.axis_index("dp"), lax.axis_index("mp")
    x, y, c = dp // (2 * NY), dp // 2 % NY, dp % 2
    z, h = mp // 2, mp % 2

    def at_x(k):
        return (((x + k) % NX * NY + y) * 2 + c, mp)

    def at_y(k):
        return ((x * NY + (y + k) % NY) * 2 + c, mp)

    def at_z(k):
        return (dp, (z + k) % NZ * 2 + h)

    at_h = (dp, z * 2 + 1 - h)
    at_core = (dp + 1 - 2 * c, mp)

    def move(source, target, name, place, device, recv_place=None):
        recv_place = place if recv_place is None else recv_place
        return pltpu.make_async_remote_copy(
            src_ref=source, dst_ref=target, send_sem=send.at[BASE[name] + place],
            recv_sem=recv.at[BASE[name] + recv_place], device_id=device, device_id_type=pl.DeviceIdType.MESH,
        )

    loads = []
    for i, (source, target) in enumerate(
        ((act_in, act), (basis_in, basis), (grads_in, grads), (first_in, first), (second_in, second))
    ):
        loads.append(pltpu.make_async_copy(source, target, load.at[i]))
        loads[-1].start()

    pending = []

    def finish():
        for wait in pending:
            wait()

    def go(copy):
        copy.start()
        pending.append(copy.wait_send)
        return copy

    barrier = pltpu.get_barrier_semaphore()
    partners = [at_x(k) for k in range(1, NX)] + [at_y(k) for k in range(1, NY)] + [at_z(k) for k in range(1, NZ)]
    partners += [at_h, at_core]
    for device in partners:
        pl.semaphore_signal(barrier, inc=1, device_id=device, device_id_type=pl.DeviceIdType.MESH)

    holds = z == x
    owns = jnp.logical_and(holds, h == y // 2)

    loads[0].wait()
    loads[1].wait()

    @pl.when(owns)
    def _():
        rows[...] = basis[pl.ds(pl.multiple_of((y % 2 * 2 + c) * 128, 128), 128), :]

    def rows_h():
        return move(rows, rows, "rows_h", 0, at_h)

    def rows_z(k):
        return move(rows, rows, "rows_z", k, at_z(k), 0)

    def columns(k):
        return pl.ds(pl.multiple_of((z + k + x) % NX * CHUNK, CHUNK), CHUNK)

    def project(k):
        return jnp.transpose(jnp.dot(act[...], basis[:, columns(k)], preferred_element_type=f32))

    def reduce_z(p, k):
        return move(part_send.at[p, k], part_recv.at[p, k], "reduce_z", p * NZ + k, at_z(k))

    for i, k in enumerate(OFFSETS):
        value = project(k).astype(bf16)
        for p in range(PARTS):
            part_send[p, k] = value[p * PART : (p + 1) * PART]
        if i == 0:
            pl.semaphore_wait(barrier, len(partners))
        go(reduce_z(0, k))
    for p in range(1, PARTS):
        for k in OFFSETS:
            go(reduce_z(p, k))

    @pl.when(owns)
    def _():
        rows_h().start()

    def sent_rows_h():
        @pl.when(owns)
        def _():
            rows_h().wait_send()

    pending.append(sent_rows_h)
    own[...] = project(0)
    pairs = []
    for p in range(PARTS):
        total = own[p * PART : (p + 1) * PART, :]
        for k in OFFSETS:
            reduce_z(p, k).wait_recv()
        for k in range(1, NZ):
            total = total + part_recv[p, k].astype(f32)
        half[p] = total
        pairs.append(go(move(half.at[p], half_recv.at[p], "pair_h", p, at_h)))

    def gather_z(p, k):
        ranks = pl.ds(p * PART, PART)
        return move(turned.at[ranks], turned_recv.at[k, ranks], "gather_z", p * NZ + k, at_z(k))

    def gather(p):
        pairs[p].wait_recv()
        turned[pl.ds(p * PART, PART), :] = (half[p] + half_recv[p]).astype(bf16)
        for k in NEAR:
            go(gather_z(p, k))

    def away(k):
        return (z - k + NZ) % NX

    def ys(p):
        return pl.ds(p * PART_Y, PART_Y)

    def to_core(p, k):
        return move(full.at[k, ys(p), 1 - c], core_recv.at[k, ys(p)], "pair_core", p * NX + k, at_core)

    def to_x(p, o):
        return move(x_send.at[o, ys(p)], x_recv.at[o, ys(p)], "first_x", p * NX + o, at_x(o))

    def to_y(q, o):
        return move(y_send.at[o, (y + q) % NY], y_recv.at[q, o], "first_y", q * NX + o, at_y(q))

    def sum_cores(p, k):
        to_core(p, k).wait_recv()
        o = away(k)
        both = full[k, ys(p), c] + core_recv[k, ys(p)]
        mine[o, ys(p)] = both
        x_send[o, ys(p)] = both[:, :, :XF].astype(bf16)
        y_send[o, ys(p)] = both[:, :, XF:].astype(bf16)

        @pl.when(o != 0)
        def _():
            to_x(p, o).start()

        for i in range(PART_Y):
            q = (p * PART_Y + i - y + NY) % NY

            @pl.when(q != 0)
            def _():
                to_y(q, o).start()

    def gradient(p, k):
        if k:
            gather_z(p, k).wait_recv()
            block = turned_recv[k, pl.ds(p * PART, PART)]
        else:
            block = turned[pl.ds(p * PART, PART), :]
        product = jnp.dot(block, grads[...], preferred_element_type=f32)
        full[k, ys(p)] = product.reshape(PART_Y, 2, ROWS, FF)
        go(to_core(p, k))

    loads[2].wait()
    work = [(p, k) for p in range(PARTS) for k in (0,) + NEAR]
    gather(0)
    for i, (p, k) in enumerate(work):
        gradient(p, k)
        if i % NZ == 0 and p + 1 < PARTS:
            gather(p + 1)
        if i >= BEHIND:
            sum_cores(*work[i - BEHIND])
    for item in work[len(work) - BEHIND :]:
        sum_cores(*item)
    for o in range(NX):
        if o:
            for p in range(PARTS):
                pending.append(to_x(p, o).wait_send)
        for q in range(1, NY):
            pending.append(to_y(q, o).wait_send)

    @pl.when(jnp.logical_and(holds, jnp.logical_not(owns)))
    def _():
        rows_h().wait_recv()

    @pl.when(holds)
    def _():
        for k in OFFSETS:
            rows_z(k).start()

    def sent_rows_z():
        @pl.when(holds)
        def _():
            for k in OFFSETS:
                rows_z(k).wait_send()

    pending.append(sent_rows_z)

    def second_x(o):
        return move(u_send.at[o], u_recv.at[o], "second_x", o, at_x(o))

    def sum_y(o):
        value = mine[o, y][:, XF:]
        for q in range(1, NY):
            value = value + y_recv[q, o].astype(f32)
        return value

    for k in (0,) + NEAR:
        o = away(k)
        for q in range(1, NY):
            to_y(q, o).wait_recv()
        u_send[o] = sum_y(o).astype(bf16)

        @pl.when(o != 0)
        def _():
            second_x(o).start()

    for o in range(1, NX):
        pending.append(second_x(o).wait_send)
    value = mine[0][:, :, :XF]
    for o in range(1, NX):
        for p in range(PARTS):
            to_x(p, o).wait_recv()
        value = value + x_recv[o].astype(f32)
    t_send[...] = value
    second_y = []
    for q in SIDES:
        second_y.append(go(move(t_send.at[(y + q) % NY], t_recv.at[q], "second_y", q, at_y(q))))

    loads[3].wait()
    loads[4].wait()

    def adam(gradient, columns, target):
        new_first = beta_first * first[:, columns] + (1.0 - beta_first) * gradient
        new_second = beta_second * second[:, columns] + (1.0 - beta_second) * gradient * gradient
        first_hat = new_first / (1.0 - beta_first**STEP)
        second_hat = new_second / (1.0 - beta_second**STEP)
        first_out[:, columns] = new_first
        second_out[:, columns] = new_second
        target[x, y, c] = (first_hat / (jnp.sqrt(second_hat) + adam_eps)).astype(bf16)

    def block(q, o):
        return (x + NX - o) % NX, (y + NY - q) % NY, c

    def to_x_one(o):
        ref = dir_one.at[x, y, c]
        return move(ref, ref, "one", o, at_x(o))

    def to_y_one(q, o):
        ref = dir_one.at[block(0, o)]
        return move(ref, ref, "one", q * NX + o, at_y(q))

    def to_y_two(q):
        ref = dir_two.at[x, y, c]
        return move(ref, ref, "two", q * NX, at_y(q))

    def to_x_two(q, o):
        ref = dir_two.at[block(q, 0)]
        return move(ref, ref, "two", q * NX + o, at_x(o))

    def share(array, name, q, o):
        ref = array.at[block(q, o)]
        return move(ref, ref, name, q * NX + o, at_core)

    def came(array, name, q, o):
        ref = array.at[block(q, o)]
        move(ref, ref, name, q * NX + o, at_x(1)).wait_recv()

    for copy in second_y:
        copy.wait_recv()
    value = t_send[y]
    for q in range(1, NY):
        value = value + t_recv[q]
    adam(value, slice(0, XF), dir_two)
    for q in SIDES:
        go(to_y_two(q))
    for o in OFFSETS:
        go(to_x_two(0, o))
    go(share(dir_two, "core_two", 0, 0))
    value = sum_y(0)
    for o in range(1, NX):
        second_x(o).wait_recv()
        value = value + u_recv[o].astype(f32)
    adam(value, slice(XF, FF), dir_one)
    for o in OFFSETS:
        go(to_x_one(o))
    for q in SIDES:
        go(to_y_one(q, 0))
    go(share(dir_one, "core_one", 0, 0))
    for q in SIDES:
        came(dir_two, "two", q, 0)
        for o in OFFSETS:
            go(to_x_two(q, o))
        go(share(dir_two, "core_two", q, 0))
    for o in NEAR:
        came(dir_one, "one", 0, o)
        for q in SIDES:
            go(to_y_one(q, o))
        go(share(dir_one, "core_one", 0, o))
    for q in (0,) + SIDES:
        for o in NEAR:
            came(dir_two, "two", q, o)
            go(share(dir_two, "core_two", q, o))
    for o in (0,) + NEAR:
        for q in SIDES:
            came(dir_one, "one", q, o)
            go(share(dir_one, "core_one", q, o))

    @pl.when(jnp.logical_not(holds))
    def _():
        rows_z(0).wait_recv()

    for q in range(NY):
        for o in range(NX):
            share(dir_two, "core_two", q, o).wait_recv()
    step_out[:, :XF] = galore_scale * jnp.dot(
        rows[...], dir_two[...].reshape(RANK, XF), preferred_element_type=f32
    )
    for q in range(NY):
        for o in range(NX):
            share(dir_one, "core_one", q, o).wait_recv()
    step_out[:, XF:] = galore_scale * jnp.dot(
        rows[...], dir_one[...].reshape(RANK, YF), preferred_element_type=f32
    )
    finish()


def body(activations, out_grads, basis, first_moment, second_moment):
    vmem = pl.BlockSpec(memory_space=pltpu.VMEM)
    return pl.pallas_call(
        kernel,
        out_shape=(
            jax.ShapeDtypeStruct((128, FF), f32),
            jax.ShapeDtypeStruct((ROWS, FF), f32),
            jax.ShapeDtypeStruct((ROWS, FF), f32),
        ),
        in_specs=[pl.BlockSpec(memory_space=pl.ANY)] * 5,
        out_specs=(vmem,) * 3,
        scratch_shapes=[
            pltpu.VMEM((TOK, 512), bf16),
            pltpu.VMEM((TOK, FF), bf16),
            pltpu.VMEM((512, RANK), bf16),
            pltpu.VMEM((ROWS, FF), f32),
            pltpu.VMEM((ROWS, FF), f32),
            pltpu.VMEM((CHUNK, TOK), f32),
            pltpu.VMEM((PARTS, NZ, PART, TOK), bf16),
            pltpu.VMEM((PARTS, NZ, PART, TOK), bf16),
            pltpu.VMEM((PARTS, PART, TOK), f32),
            pltpu.VMEM((PARTS, PART, TOK), f32),
            pltpu.VMEM((CHUNK, TOK), bf16),
            pltpu.VMEM((NZ, CHUNK, TOK), bf16),
            pltpu.VMEM((NX, NY, 2, ROWS, FF), f32),
            pltpu.VMEM((NX, NY, ROWS, FF), f32),
            pltpu.VMEM((NX, NY, ROWS, FF), f32),
            pltpu.VMEM((NX, NY, ROWS, XF), bf16),
            pltpu.VMEM((NX, NY, ROWS, XF), bf16),
            pltpu.VMEM((NX, NY, ROWS, YF), bf16),
            pltpu.VMEM((NY, NX, ROWS, YF), bf16),
            pltpu.VMEM((NY, ROWS, XF), f32),
            pltpu.VMEM((NY, ROWS, XF), f32),
            pltpu.VMEM((NX, ROWS, YF), bf16),
            pltpu.VMEM((NX, ROWS, YF), bf16),
            pltpu.VMEM((NX, NY, 2, ROWS, YF), bf16),
            pltpu.VMEM((NX, NY, 2, ROWS, XF), bf16),
            pltpu.VMEM((128, RANK), bf16),
            pltpu.SemaphoreType.DMA((SEMS,)),
            pltpu.SemaphoreType.DMA((SEMS,)),
            pltpu.SemaphoreType.DMA((5,)),
        ],
        compiler_params=pltpu.CompilerParams(
            collective_id=0, has_side_effects=True, vmem_limit_bytes=60 << 20
        ),
        cost_estimate=pl.CostEstimate(flops=10**9, bytes_accessed=4 << 20, transcendentals=0),
        name="galore_step",
    )(activations, out_grads, basis, first_moment, second_moment)


def solution(mesh):
    return jax.shard_map(
        body,
        mesh=mesh,
        in_specs=(P("dp", "mp"), P("dp", "mp"), P("mp", None), P("dp", "mp"), P("dp", "mp")),
        out_specs=(P("dp", "mp"), P("dp", "mp"), P("dp", "mp")),
        check_vma=False,
    )
```

```python
import jax
import jax.numpy as jnp
from jax import lax
from jax.experimental import pallas as pl
from jax.experimental.pallas import tpu as pltpu
from jax.sharding import PartitionSpec as P

STEP = 10

beta_first = 0.9
beta_second = 0.95
adam_eps = 1e-08
galore_scale = 0.25

NX, NY, NZ = 8, 4, 8
RANK = 1024
TOK = 256
FF = 896
CHUNK = RANK // NX
PARTS = 2
PART = CHUNK // PARTS
PART_Y = NY // PARTS
BEHIND = 3
ROWS = 16
XF = 384
YF = FF - XF
OFFSETS = (4, 3, 5, 2, 6, 1, 7)
NEAR = (1, 7, 2, 6, 3, 5, 4)
SIDES = (1, 3, 2)

f32, bf16 = jnp.float32, jnp.bfloat16

EXCHANGES = {
    "reduce_z": (1, PARTS), "pair_h": (1, PARTS), "gather_z": (1, PARTS * NZ), "pair_core": (1, PARTS * NX),
    "first_x": (1, 1), "first_y": (1, NX), "second_y": (1, 1), "second_x": (1, 1),
    "x_one": (1, NX), "y_one": (1, NX), "y_two": (1, NY), "x_two": (1, NX), "core_one": (1, 1), "core_two": (1, 1),
    "rows_h": (1, 1), "rows_z": (2, 1),
}
SENDS, RECVS, BASE = 0, 0, {}
for name, (sends, recvs) in EXCHANGES.items():
    BASE[name] = (SENDS, RECVS)
    SENDS, RECVS = SENDS + sends, RECVS + recvs


def kernel(
    act_in, grads_in, basis_in, first_in, second_in, step_out, first_out, second_out,
    act, grads, basis, first, second,
    own, part_send, part_recv, half, half_recv, turned, turned_recv, full, core_recv, mine, x_send, x_recv,
    y_send, y_recv, t_send, t_recv, u_send, u_recv, dir_one, dir_two, rows, send, recv, load,
):
    dp, mp = lax.axis_index("dp"), lax.axis_index("mp")
    x, y, c = dp // (2 * NY), dp // 2 % NY, dp % 2
    z, h = mp // 2, mp % 2

    def at_x(k):
        return (((x + k) % NX * NY + y) * 2 + c, mp)

    def at_y(k):
        return ((x * NY + (y + k) % NY) * 2 + c, mp)

    def at_z(k):
        return (dp, (z + k) % NZ * 2 + h)

    at_h = (dp, z * 2 + 1 - h)
    at_core = (dp + 1 - 2 * c, mp)

    def move(source, target, name, device, place=0, send_place=0):
        return pltpu.make_async_remote_copy(
            src_ref=source, dst_ref=target, send_sem=send.at[BASE[name][0] + send_place],
            recv_sem=recv.at[BASE[name][1] + place], device_id=device, device_id_type=pl.DeviceIdType.MESH,
        )

    def arrived(ref, name, place=0):
        move(ref, ref, name, at_core, place).wait_recv()

    def left_here(ref, name):
        pending.append(move(ref, ref, name, at_core).wait_send)

    others = pl.ds(1, NX - 1)
    others_y = pl.ds(1, NY - 1)

    loads = []
    for i, (source, target) in enumerate(
        ((act_in, act), (basis_in, basis), (grads_in, grads), (first_in, first), (second_in, second))
    ):
        loads.append(pltpu.make_async_copy(source, target, load.at[i]))
    loads[0].start()
    loads[1].start()

    pending = []

    def finish():
        for wait in pending:
            wait()

    barrier = pltpu.get_barrier_semaphore()
    partners = [at_x(k) for k in range(1, NX)] + [at_y(k) for k in range(1, NY)] + [at_z(k) for k in range(1, NZ)]
    partners += [at_h, at_core]
    for device in partners:
        pl.semaphore_signal(barrier, inc=1, device_id=device, device_id_type=pl.DeviceIdType.MESH)

    holds = z == x
    owns = jnp.logical_and(holds, h == y // 2)

    loads[0].wait()
    loads[1].wait()

    @pl.when(owns)
    def _():
        rows[...] = basis[pl.ds(pl.multiple_of((y % 2 * 2 + c) * 128, 128), 128), :]

    def rows_h():
        return move(rows, rows, "rows_h", at_h)

    right, left = (z - x + NZ) % NZ, (x - z + NZ) % NZ

    def rows_z(way):
        return move(rows, rows, "rows_z", at_z(1 if way == 0 else NZ - 1), 0, way)

    def pass_rows(step):
        for way, hops in enumerate((right, left)):
            if step < NZ // 2 - way:

                @pl.when(hops == step)
                def _():
                    if step:
                        rows_z(0).wait_recv()
                    rows_z(way).start()

    def columns(k):
        return pl.ds(pl.multiple_of((z + k + x) % NX * CHUNK, CHUNK), CHUNK)

    def project(k):
        return jnp.transpose(jnp.dot(act[...], basis[:, columns(k)], preferred_element_type=f32))

    def reduce_z(p, k):
        return move(part_send.at[p, k], part_recv.at[p, k], "reduce_z", at_z(k), p)

    for i, k in enumerate(OFFSETS):
        value = project(k).astype(bf16)
        for p in range(PARTS):
            part_send[p, k] = value[p * PART : (p + 1) * PART]
        if i == 0:
            pl.semaphore_wait(barrier, len(partners))
        reduce_z(0, k).start()
    for p in range(1, PARTS):
        for k in OFFSETS:
            reduce_z(p, k).start()
    left_here(part_send.at[:, others], "reduce_z")
    for copy in loads[2:]:
        copy.start()

    @pl.when(owns)
    def _():
        rows_h().start()

    def sent_rows_h():
        @pl.when(owns)
        def _():
            rows_h().wait_send()

    pending.append(sent_rows_h)
    def pair_h(p):
        return move(half.at[p], half_recv.at[p], "pair_h", at_h, p)

    own[...] = project(0)
    for p in range(PARTS):
        total = own[p * PART : (p + 1) * PART, :]
        arrived(part_recv.at[p, others], "reduce_z", p)
        for k in range(1, NZ):
            total = total + part_recv[p, k].astype(f32)
        half[p] = total
        pair_h(p).start()
    left_here(half, "pair_h")

    def gather_z(p, k):
        ranks = pl.ds(p * PART, PART)
        return move(turned.at[ranks], turned_recv.at[k, ranks], "gather_z", at_z(k), p * NZ + k)

    def gather(p):
        pair_h(p).wait_recv()
        turned[pl.ds(p * PART, PART), :] = (half[p] + half_recv[p]).astype(bf16)
        for k in NEAR:
            gather_z(p, k).start()

    def away(k):
        return (z - k + NZ) % NX

    def ys(p):
        return pl.ds(p * PART_Y, PART_Y)

    def to_core(p, k):
        return move(full.at[k, ys(p), 1 - c], core_recv.at[k, ys(p)], "pair_core", at_core, p * NX + k)

    def to_x(p, o):
        return move(x_send.at[o, ys(p)], x_recv.at[o, ys(p)], "first_x", at_x(o))

    def to_y(q, o):
        return move(y_send.at[o, (y + q) % NY], y_recv.at[q, o], "first_y", at_y(q), o)

    def sum_cores(p, k):
        to_core(p, k).wait_recv()
        o = away(k)
        both = full[k, ys(p), c] + core_recv[k, ys(p)]
        mine[o, ys(p)] = both
        x_send[o, ys(p)] = both[:, :, :XF].astype(bf16)
        y_send[o, ys(p)] = both[:, :, XF:].astype(bf16)

        @pl.when(o != 0)
        def _():
            to_x(p, o).start()

        for i in range(PART_Y):
            q = (p * PART_Y + i - y + NY) % NY

            @pl.when(q != 0)
            def _():
                to_y(q, o).start()

    def gradient(p, k):
        if k:
            gather_z(p, k).wait_recv()
            block = turned_recv[k, pl.ds(p * PART, PART)]
        else:
            block = turned[pl.ds(p * PART, PART), :]
        product = jnp.dot(block, grads[...], preferred_element_type=f32)
        full[k, ys(p)] = product.reshape(PART_Y, 2, ROWS, FF)
        to_core(p, k).start()

    loads[2].wait()
    work = [(p, k) for p in range(PARTS) for k in (0,) + NEAR]
    gather(0)
    for i, (p, k) in enumerate(work):
        gradient(p, k)
        if i % NZ == 0 and p + 1 < PARTS:
            gather(p + 1)
        if i >= BEHIND:
            sum_cores(*work[i - BEHIND])
    for item in work[len(work) - BEHIND :]:
        sum_cores(*item)
    left_here(turned_recv.at[others], "gather_z")
    left_here(core_recv, "pair_core")
    left_here(x_send.at[others], "first_x")
    left_here(y_recv.at[others_y], "first_y")

    @pl.when(jnp.logical_and(holds, jnp.logical_not(owns)))
    def _():
        rows_h().wait_recv()

    pass_rows(0)

    def sent_rows_z():
        for way, hops in enumerate((right, left)):

            @pl.when(hops < NZ // 2 - way)
            def _():
                rows_z(way).wait_send()

    pending.append(sent_rows_z)

    def second_x(o):
        return move(u_send.at[o], u_recv.at[o], "second_x", at_x(o))

    def sum_y(o):
        value = mine[o, y][:, XF:]
        for q in range(1, NY):
            value = value + y_recv[q, o].astype(f32)
        return value

    for k in (0,) + NEAR:
        o = away(k)
        arrived(y_recv.at[others_y, o], "first_y", o)
        u_send[o] = sum_y(o).astype(bf16)

        @pl.when(o != 0)
        def _():
            second_x(o).start()

    left_here(u_send.at[others], "second_x")
    arrived(x_recv.at[others], "first_x")
    value = mine[0][:, :, :XF]
    for o in range(1, NX):
        value = value + x_recv[o].astype(f32)
    t_send[...] = value
    for q in SIDES:
        move(t_send.at[(y + q) % NY], t_recv.at[q], "second_y", at_y(q)).start()
    left_here(t_recv.at[others_y], "second_y")

    pass_rows(1)
    loads[3].wait()
    loads[4].wait()

    def adam(gradient, columns, target):
        new_first = beta_first * first[:, columns] + (1.0 - beta_first) * gradient
        new_second = beta_second * second[:, columns] + (1.0 - beta_second) * gradient * gradient
        first_hat = new_first / (1.0 - beta_first**STEP)
        second_hat = new_second / (1.0 - beta_second**STEP)
        first_out[:, columns] = new_first
        second_out[:, columns] = new_second
        target[x, y, c] = (first_hat / (jnp.sqrt(second_hat) + adam_eps)).astype(bf16)

    def x_from(o):
        return (x + NX - o) % NX

    def y_from(q):
        return (y + NY - q) % NY

    def x_one(o):
        ref = dir_one.at[x, y, c]
        return move(ref, ref, "x_one", at_x(o), o)

    def y_one(q, o):
        ref = dir_one.at[x_from(o), y, c]
        return move(ref, ref, "y_one", at_y(q), o)

    def y_two(q):
        ref = dir_two.at[x, y, c]
        return move(ref, ref, "y_two", at_y(q), q)

    def x_two(q, o):
        ref = dir_two.at[x, y_from(q), c]
        return move(ref, ref, "x_two", at_x(o), o)

    def share(array, name, o):
        ref = array.at[x_from(o), :, c]
        return move(ref, ref, name, at_core)

    arrived(t_recv.at[others_y], "second_y")
    value = t_send[y]
    for q in range(1, NY):
        value = value + t_recv[q]
    adam(value, slice(0, XF), dir_two)
    for q in SIDES:
        y_two(q).start()
    for o in OFFSETS:
        x_two(0, o).start()
    pass_rows(2)
    arrived(u_recv.at[others], "second_x")
    value = sum_y(0)
    for o in range(1, NX):
        value = value + u_recv[o].astype(f32)
    adam(value, slice(XF, FF), dir_one)
    for o in OFFSETS:
        x_one(o).start()
    for q in SIDES:
        y_one(q, 0).start()
    pass_rows(3)
    for q in SIDES:
        y_two(q).wait_recv()
        for o in OFFSETS:
            x_two(q, o).start()
    share(dir_two, "core_two", 0).start()
    for o in NEAR:
        x_one(o).wait_recv()
        for q in SIDES:
            y_one(q, o).start()
    for o in NEAR:
        arrived(dir_two.at[x_from(o), :, c], "x_two", o)
        share(dir_two, "core_two", o).start()
    for o in (0,) + NEAR:
        arrived(dir_one.at[x_from(o), pl.ds(0, NY - 1), c], "y_one", o)
        share(dir_one, "core_one", o).start()
    left_here(dir_one.at[others, 0, c], "x_one")
    left_here(dir_one.at[:, pl.ds(0, NY - 1), c], "y_one")
    left_here(dir_two.at[0, pl.ds(0, NY - 1), c], "y_two")
    left_here(dir_two.at[others, :, c], "x_two")
    left_here(dir_one.at[:, :, c], "core_one")
    left_here(dir_two.at[:, :, c], "core_two")

    @pl.when(jnp.logical_or(right == NZ // 2, left == NZ // 2 - 1))
    def _():
        rows_z(0).wait_recv()

    arrived(dir_two.at[:, :, 1 - c], "core_two")
    step_out[:, :XF] = galore_scale * jnp.dot(
        rows[...], dir_two[...].reshape(RANK, XF), preferred_element_type=f32
    )
    arrived(dir_one.at[:, :, 1 - c], "core_one")
    step_out[:, XF:] = galore_scale * jnp.dot(
        rows[...], dir_one[...].reshape(RANK, YF), preferred_element_type=f32
    )
    finish()


def body(activations, out_grads, basis, first_moment, second_moment):
    vmem = pl.BlockSpec(memory_space=pltpu.VMEM)
    return pl.pallas_call(
        kernel,
        out_shape=(
            jax.ShapeDtypeStruct((128, FF), f32),
            jax.ShapeDtypeStruct((ROWS, FF), f32),
            jax.ShapeDtypeStruct((ROWS, FF), f32),
        ),
        in_specs=[pl.BlockSpec(memory_space=pl.ANY)] * 5,
        out_specs=(vmem,) * 3,
        scratch_shapes=[
            pltpu.VMEM((TOK, 512), bf16),
            pltpu.VMEM((TOK, FF), bf16),
            pltpu.VMEM((512, RANK), bf16),
            pltpu.VMEM((ROWS, FF), f32),
            pltpu.VMEM((ROWS, FF), f32),
            pltpu.VMEM((CHUNK, TOK), f32),
            pltpu.VMEM((PARTS, NZ, PART, TOK), bf16),
            pltpu.VMEM((PARTS, NZ, PART, TOK), bf16),
            pltpu.VMEM((PARTS, PART, TOK), f32),
            pltpu.VMEM((PARTS, PART, TOK), f32),
            pltpu.VMEM((CHUNK, TOK), bf16),
            pltpu.VMEM((NZ, CHUNK, TOK), bf16),
            pltpu.VMEM((NX, NY, 2, ROWS, FF), f32),
            pltpu.VMEM((NX, NY, ROWS, FF), f32),
            pltpu.VMEM((NX, NY, ROWS, FF), f32),
            pltpu.VMEM((NX, NY, ROWS, XF), bf16),
            pltpu.VMEM((NX, NY, ROWS, XF), bf16),
            pltpu.VMEM((NX, NY, ROWS, YF), bf16),
            pltpu.VMEM((NY, NX, ROWS, YF), bf16),
            pltpu.VMEM((NY, ROWS, XF), f32),
            pltpu.VMEM((NY, ROWS, XF), f32),
            pltpu.VMEM((NX, ROWS, YF), bf16),
            pltpu.VMEM((NX, ROWS, YF), bf16),
            pltpu.VMEM((NX, NY, 2, ROWS, YF), bf16),
            pltpu.VMEM((NX, NY, 2, ROWS, XF), bf16),
            pltpu.VMEM((128, RANK), bf16),
            pltpu.SemaphoreType.DMA((SENDS,)),
            pltpu.SemaphoreType.DMA((RECVS,)),
            pltpu.SemaphoreType.DMA((5,)),
        ],
        compiler_params=pltpu.CompilerParams(
            collective_id=0, has_side_effects=True, vmem_limit_bytes=60 << 20
        ),
        cost_estimate=pl.CostEstimate(flops=10**9, bytes_accessed=4 << 20, transcendentals=0),
        name="galore_step",
    )(activations, out_grads, basis, first_moment, second_moment)


def solution(mesh):
    return jax.shard_map(
        body,
        mesh=mesh,
        in_specs=(P("dp", "mp"), P("dp", "mp"), P("mp", None), P("dp", "mp"), P("dp", "mp")),
        out_specs=(P("dp", "mp"), P("dp", "mp"), P("dp", "mp")),
        check_vma=False,
    )
```

```python
import jax
import jax.numpy as jnp
from jax import lax
from jax.experimental import pallas as pl
from jax.experimental.pallas import tpu as pltpu
from jax.sharding import PartitionSpec as P

STEP = 10

beta_first = 0.9
beta_second = 0.95
adam_eps = 1e-08
galore_scale = 0.25

NX, NY, NZ = 8, 4, 8
RANK = 1024
TOK = 256
FF = 896
CHUNK = RANK // NX
PARTS = 2
PART = CHUNK // PARTS
BEHIND = 3
ROWS = 16
XF = 384
YF = FF - XF
OFFSETS = (4, 3, 5, 2, 6, 1, 7)
NEAR = (1, 7, 2, 6, 3, 5, 4)
SIDES = (1, 3, 2)

f32, bf16 = jnp.float32, jnp.bfloat16

EXCHANGES = {
    "reduce_z": (1, PARTS), "pair_h": (1, PARTS), "gather_z": (1, PARTS * NZ), "pair_core": (1, NX),
    "first_x": (1, 1), "first_y": (1, NX), "second_y": (1, 1), "second_x": (1, 1),
    "x_one": (1, NX), "y_one": (1, NX), "y_two": (1, NY), "x_two": (1, NX), "core_one": (1, 1), "core_two": (1, 1),
    "rows_h": (1, 1), "rows_z": (2, 1),
}
SENDS, RECVS, BASE = 0, 0, {}
for name, (sends, recvs) in EXCHANGES.items():
    BASE[name] = (SENDS, RECVS)
    SENDS, RECVS = SENDS + sends, RECVS + recvs


def kernel(
    act_in, grads_in, basis_in, first_in, second_in, step_out, first_out, second_out,
    act, grads, basis, first, second,
    own, part_send, part_recv, half, half_recv, turned, turned_recv, full, core_recv, mine, x_send, x_recv,
    y_send, y_recv, t_send, t_recv, u_send, u_recv, dir_one, dir_two, rows, send, recv, load,
):
    dp, mp = lax.axis_index("dp"), lax.axis_index("mp")
    x, y, c = dp // (2 * NY), dp // 2 % NY, dp % 2
    z, h = mp // 2, mp % 2

    def at_x(k):
        return (((x + k) % NX * NY + y) * 2 + c, mp)

    def at_y(k):
        return ((x * NY + (y + k) % NY) * 2 + c, mp)

    def at_z(k):
        return (dp, (z + k) % NZ * 2 + h)

    at_h = (dp, z * 2 + 1 - h)
    at_core = (dp + 1 - 2 * c, mp)

    def move(source, target, name, device, place=0, send_place=0):
        return pltpu.make_async_remote_copy(
            src_ref=source, dst_ref=target, send_sem=send.at[BASE[name][0] + send_place],
            recv_sem=recv.at[BASE[name][1] + place], device_id=device, device_id_type=pl.DeviceIdType.MESH,
        )

    def arrived(ref, name, place=0):
        move(ref, ref, name, at_core, place).wait_recv()

    def left_here(ref, name):
        pending.append(move(ref, ref, name, at_core).wait_send)

    others = pl.ds(1, NX - 1)
    others_y = pl.ds(1, NY - 1)

    loads = []
    for i, (source, target) in enumerate(
        ((act_in, act), (basis_in, basis), (grads_in, grads), (first_in, first), (second_in, second))
    ):
        loads.append(pltpu.make_async_copy(source, target, load.at[i]))
    loads[0].start()
    loads[1].start()

    pending = []

    def finish():
        for wait in pending:
            wait()

    barrier = pltpu.get_barrier_semaphore()
    partners = [at_x(k) for k in range(1, NX)] + [at_y(k) for k in range(1, NY)] + [at_z(k) for k in range(1, NZ)]
    partners += [at_h, at_core]
    for device in partners:
        pl.semaphore_signal(barrier, inc=1, device_id=device, device_id_type=pl.DeviceIdType.MESH)

    holds = z == x
    owns = jnp.logical_and(holds, h == y // 2)

    loads[0].wait()
    loads[1].wait()

    @pl.when(owns)
    def _():
        rows[...] = basis[pl.ds(pl.multiple_of((y % 2 * 2 + c) * 128, 128), 128), :]

    def rows_h():
        return move(rows, rows, "rows_h", at_h)

    right, left = (z - x + NZ) % NZ, (x - z + NZ) % NZ

    def rows_z(way):
        return move(rows, rows, "rows_z", at_z(1 if way == 0 else NZ - 1), 0, way)

    def pass_rows(step):
        for way, hops in enumerate((right, left)):
            if step < NZ // 2 - way:

                @pl.when(hops == step)
                def _():
                    if step:
                        rows_z(0).wait_recv()
                    rows_z(way).start()

    def columns(k):
        return pl.ds(pl.multiple_of((z + k + x) % NX * CHUNK, CHUNK), CHUNK)

    def project(k):
        value = jnp.transpose(jnp.dot(act[...], basis[:, columns(k)], preferred_element_type=f32))
        value = value.reshape(NY, PARTS, ROWS, TOK)
        return [value[:, p].reshape(PART, TOK) for p in range(PARTS)]

    def reduce_z(p, k):
        return move(part_send.at[p, k], part_recv.at[p, k], "reduce_z", at_z(k), p)

    for i, k in enumerate(OFFSETS):
        for p, value in enumerate(project(k)):
            part_send[p, k] = value.astype(bf16)
        if i == 0:
            pl.semaphore_wait(barrier, len(partners))
        reduce_z(0, k).start()
    for p in range(1, PARTS):
        for k in OFFSETS:
            reduce_z(p, k).start()
    left_here(part_send.at[:, others], "reduce_z")
    for copy in loads[2:]:
        copy.start()

    @pl.when(owns)
    def _():
        rows_h().start()

    def sent_rows_h():
        @pl.when(owns)
        def _():
            rows_h().wait_send()

    pending.append(sent_rows_h)
    def pair_h(p):
        return move(half.at[p], half_recv.at[p], "pair_h", at_h, p)

    for p, value in enumerate(project(0)):
        own[p] = value
    for p in range(PARTS):
        total = own[p]
        arrived(part_recv.at[p, others], "reduce_z", p)
        for k in range(1, NZ):
            total = total + part_recv[p, k].astype(f32)
        half[p] = total
        pair_h(p).start()
    left_here(half, "pair_h")

    def gather_z(p, k):
        ranks = pl.ds(p * PART, PART)
        return move(turned.at[ranks], turned_recv.at[k, ranks], "gather_z", at_z(k), p * NZ + k)

    def gather(p):
        pair_h(p).wait_recv()
        turned[pl.ds(p * PART, PART), :] = (half[p] + half_recv[p]).astype(bf16)
        for k in NEAR:
            gather_z(p, k).start()

    def away(k):
        return (z - k + NZ) % NX

    def to_core(p, k):
        return move(full.at[k, p], core_recv.at[k], "pair_core", at_core, k)

    def to_x(o):
        return move(x_send.at[o], x_recv.at[o], "first_x", at_x(o))

    def to_y(q, o):
        return move(y_send.at[o, (y + q) % NY], y_recv.at[q, o], "first_y", at_y(q), o)

    def sum_cores(p, k):
        @pl.when(c == p)
        def _():
            to_core(p, k).wait_recv()
            o = away(k)
            both = full[k, p] + core_recv[k]
            mine[o] = both
            x_send[o] = both[:, :, :XF].astype(bf16)
            y_send[o] = both[:, :, XF:].astype(bf16)

            @pl.when(o != 0)
            def _():
                to_x(o).start()

            for q in SIDES:
                to_y(q, o).start()

    def gradient(p, k):
        if k:
            gather_z(p, k).wait_recv()
            block = turned_recv[k, pl.ds(p * PART, PART)]
        else:
            block = turned[pl.ds(p * PART, PART), :]
        product = jnp.dot(block, grads[...], preferred_element_type=f32)
        full[k, p] = product.reshape(NY, ROWS, FF)

        @pl.when(c != p)
        def _():
            to_core(p, k).start()

    loads[2].wait()
    work = [(p, k) for p in range(PARTS) for k in (0,) + NEAR]
    gather(0)
    for i, (p, k) in enumerate(work):
        gradient(p, k)
        if i % NZ == 0 and p + 1 < PARTS:
            gather(p + 1)
        if i >= BEHIND:
            sum_cores(*work[i - BEHIND])
    for item in work[len(work) - BEHIND :]:
        sum_cores(*item)
    left_here(turned_recv.at[others], "gather_z")
    left_here(core_recv, "pair_core")
    left_here(x_send.at[others], "first_x")
    left_here(y_recv.at[others_y], "first_y")

    @pl.when(jnp.logical_and(holds, jnp.logical_not(owns)))
    def _():
        rows_h().wait_recv()

    pass_rows(0)

    def sent_rows_z():
        for way, hops in enumerate((right, left)):

            @pl.when(hops < NZ // 2 - way)
            def _():
                rows_z(way).wait_send()

    pending.append(sent_rows_z)

    def second_x(o):
        return move(u_send.at[o], u_recv.at[o], "second_x", at_x(o))

    def sum_y(o):
        value = mine[o, y][:, XF:]
        for q in range(1, NY):
            value = value + y_recv[q, o].astype(f32)
        return value

    for k in (0,) + NEAR:
        o = away(k)
        arrived(y_recv.at[others_y, o], "first_y", o)
        u_send[o] = sum_y(o).astype(bf16)

        @pl.when(o != 0)
        def _():
            second_x(o).start()

    left_here(u_send.at[others], "second_x")
    arrived(x_recv.at[others], "first_x")
    value = mine[0][:, :, :XF]
    for o in range(1, NX):
        value = value + x_recv[o].astype(f32)
    t_send[...] = value
    for q in SIDES:
        move(t_send.at[(y + q) % NY], t_recv.at[q], "second_y", at_y(q)).start()
    left_here(t_recv.at[others_y], "second_y")

    pass_rows(1)
    loads[3].wait()
    loads[4].wait()

    def adam(gradient, columns, target):
        new_first = beta_first * first[:, columns] + (1.0 - beta_first) * gradient
        new_second = beta_second * second[:, columns] + (1.0 - beta_second) * gradient * gradient
        first_hat = new_first / (1.0 - beta_first**STEP)
        second_hat = new_second / (1.0 - beta_second**STEP)
        first_out[:, columns] = new_first
        second_out[:, columns] = new_second
        target[x, y, c] = (first_hat / (jnp.sqrt(second_hat) + adam_eps)).astype(bf16)

    def x_from(o):
        return (x + NX - o) % NX

    def y_from(q):
        return (y + NY - q) % NY

    def x_one(o):
        ref = dir_one.at[x, y, c]
        return move(ref, ref, "x_one", at_x(o), o)

    def y_one(q, o):
        ref = dir_one.at[x_from(o), y, c]
        return move(ref, ref, "y_one", at_y(q), o)

    def y_two(q):
        ref = dir_two.at[x, y, c]
        return move(ref, ref, "y_two", at_y(q), q)

    def x_two(q, o):
        ref = dir_two.at[x, y_from(q), c]
        return move(ref, ref, "x_two", at_x(o), o)

    def share(array, name, o):
        ref = array.at[x_from(o), :, c]
        return move(ref, ref, name, at_core)

    arrived(t_recv.at[others_y], "second_y")
    value = t_send[y]
    for q in range(1, NY):
        value = value + t_recv[q]
    adam(value, slice(0, XF), dir_two)
    for q in SIDES:
        y_two(q).start()
    for o in OFFSETS:
        x_two(0, o).start()
    pass_rows(2)
    arrived(u_recv.at[others], "second_x")
    value = sum_y(0)
    for o in range(1, NX):
        value = value + u_recv[o].astype(f32)
    adam(value, slice(XF, FF), dir_one)
    for o in OFFSETS:
        x_one(o).start()
    for q in SIDES:
        y_one(q, 0).start()
    pass_rows(3)
    for q in SIDES:
        y_two(q).wait_recv()
        for o in OFFSETS:
            x_two(q, o).start()
    share(dir_two, "core_two", 0).start()
    for o in NEAR:
        x_one(o).wait_recv()
        for q in SIDES:
            y_one(q, o).start()
    for o in NEAR:
        arrived(dir_two.at[x_from(o), :, c], "x_two", o)
        share(dir_two, "core_two", o).start()
    for o in (0,) + NEAR:
        arrived(dir_one.at[x_from(o), pl.ds(0, NY - 1), c], "y_one", o)
        share(dir_one, "core_one", o).start()
    left_here(dir_one.at[others, 0, c], "x_one")
    left_here(dir_one.at[:, pl.ds(0, NY - 1), c], "y_one")
    left_here(dir_two.at[0, pl.ds(0, NY - 1), c], "y_two")
    left_here(dir_two.at[others, :, c], "x_two")
    left_here(dir_one.at[:, :, c], "core_one")
    left_here(dir_two.at[:, :, c], "core_two")

    @pl.when(jnp.logical_or(right == NZ // 2, left == NZ // 2 - 1))
    def _():
        rows_z(0).wait_recv()

    arrived(dir_two.at[:, :, 1 - c], "core_two")
    step_out[:, :XF] = galore_scale * jnp.dot(
        rows[...], dir_two[...].reshape(RANK, XF), preferred_element_type=f32
    )
    arrived(dir_one.at[:, :, 1 - c], "core_one")
    step_out[:, XF:] = galore_scale * jnp.dot(
        rows[...], dir_one[...].reshape(RANK, YF), preferred_element_type=f32
    )
    finish()


def body(activations, out_grads, basis, first_moment, second_moment):
    vmem = pl.BlockSpec(memory_space=pltpu.VMEM)
    return pl.pallas_call(
        kernel,
        out_shape=(
            jax.ShapeDtypeStruct((128, FF), f32),
            jax.ShapeDtypeStruct((ROWS, FF), f32),
            jax.ShapeDtypeStruct((ROWS, FF), f32),
        ),
        in_specs=[pl.BlockSpec(memory_space=pl.ANY)] * 5,
        out_specs=(vmem,) * 3,
        scratch_shapes=[
            pltpu.VMEM((TOK, 512), bf16),
            pltpu.VMEM((TOK, FF), bf16),
            pltpu.VMEM((512, RANK), bf16),
            pltpu.VMEM((ROWS, FF), f32),
            pltpu.VMEM((ROWS, FF), f32),
            pltpu.VMEM((PARTS, PART, TOK), f32),
            pltpu.VMEM((PARTS, NZ, PART, TOK), bf16),
            pltpu.VMEM((PARTS, NZ, PART, TOK), bf16),
            pltpu.VMEM((PARTS, PART, TOK), f32),
            pltpu.VMEM((PARTS, PART, TOK), f32),
            pltpu.VMEM((CHUNK, TOK), bf16),
            pltpu.VMEM((NZ, CHUNK, TOK), bf16),
            pltpu.VMEM((NX, PARTS, NY, ROWS, FF), f32),
            pltpu.VMEM((NX, NY, ROWS, FF), f32),
            pltpu.VMEM((NX, NY, ROWS, FF), f32),
            pltpu.VMEM((NX, NY, ROWS, XF), bf16),
            pltpu.VMEM((NX, NY, ROWS, XF), bf16),
            pltpu.VMEM((NX, NY, ROWS, YF), bf16),
            pltpu.VMEM((NY, NX, ROWS, YF), bf16),
            pltpu.VMEM((NY, ROWS, XF), f32),
            pltpu.VMEM((NY, ROWS, XF), f32),
            pltpu.VMEM((NX, ROWS, YF), bf16),
            pltpu.VMEM((NX, ROWS, YF), bf16),
            pltpu.VMEM((NX, NY, 2, ROWS, YF), bf16),
            pltpu.VMEM((NX, NY, 2, ROWS, XF), bf16),
            pltpu.VMEM((128, RANK), bf16),
            pltpu.SemaphoreType.DMA((SENDS,)),
            pltpu.SemaphoreType.DMA((RECVS,)),
            pltpu.SemaphoreType.DMA((5,)),
        ],
        compiler_params=pltpu.CompilerParams(
            collective_id=0, has_side_effects=True, vmem_limit_bytes=60 << 20
        ),
        cost_estimate=pl.CostEstimate(flops=10**9, bytes_accessed=4 << 20, transcendentals=0),
        name="galore_step",
    )(activations, out_grads, basis, first_moment, second_moment)


def solution(mesh):
    return jax.shard_map(
        body,
        mesh=mesh,
        in_specs=(P("dp", "mp"), P("dp", "mp"), P("mp", None), P("dp", "mp"), P("dp", "mp")),
        out_specs=(P("dp", "mp"), P("dp", "mp"), P("dp", "mp")),
        check_vma=False,
    )
```

```python
import jax
import jax.numpy as jnp
from jax import lax
from jax.experimental import pallas as pl
from jax.experimental.pallas import tpu as pltpu
from jax.sharding import PartitionSpec as P

STEP = 10

beta_first = 0.9
beta_second = 0.95
adam_eps = 1e-08
galore_scale = 0.25

NX, NY, NZ = 8, 4, 8
RANK = 1024
TOK = 256
FF = 896
CHUNK = RANK // NX
PARTS = 2
PART = CHUNK // PARTS
BEHIND = 3
ROWS = 16
XF = 384
YF = FF - XF
OFFSETS = (4, 3, 5, 2, 6, 1, 7)
NEAR = (1, 7, 2, 6, 3, 5, 4)
SIDES = (1, 3, 2)
RELAY = (3, 5)
GATHER = ((1, 7, 3, 2, 6, 5, 4), (1, 7, 5, 2, 6, 3, 4))

f32, bf16 = jnp.float32, jnp.bfloat16

EXCHANGES = {
    "reduce_z": (1, PARTS), "pair_h": (1, PARTS), "gather_z": (1, PARTS * NZ), "pair_core": (1, NX),
    "first_x": (1, 1), "first_y": (1, NX), "second_y": (1, 1), "second_x": (1, 1),
    "x_one": (1, NX), "y_one": (1, NX), "y_two": (1, NY), "x_two": (1, NX), "core_one": (1, 1), "core_two": (1, 1),
    "rows_h": (1, 1), "rows_z": (2, 1),
}
SENDS, RECVS, BASE = 0, 0, {}
for name, (sends, recvs) in EXCHANGES.items():
    BASE[name] = (SENDS, RECVS)
    SENDS, RECVS = SENDS + sends, RECVS + recvs


def kernel(
    act_in, grads_in, basis_in, first_in, second_in, step_out, first_out, second_out,
    act, grads, basis, first, second,
    own, part_send, part_recv, half, half_recv, turned, turned_recv, full, core_recv, mine, x_send, x_recv,
    y_send, y_recv, t_send, t_recv, u_send, u_recv, dir_one, dir_two, rows, send, recv, load,
):
    dp, mp = lax.axis_index("dp"), lax.axis_index("mp")
    x, y, c = dp // (2 * NY), dp // 2 % NY, dp % 2
    z, h = mp // 2, mp % 2

    def at_x(k):
        return (((x + k) % NX * NY + y) * 2 + c, mp)

    def at_y(k):
        return ((x * NY + (y + k) % NY) * 2 + c, mp)

    def at_z(k):
        return (dp, (z + k) % NZ * 2 + h)

    at_h = (dp, z * 2 + 1 - h)
    at_core = (dp + 1 - 2 * c, mp)

    def move(source, target, name, device, place=0, send_place=0):
        return pltpu.make_async_remote_copy(
            src_ref=source, dst_ref=target, send_sem=send.at[BASE[name][0] + send_place],
            recv_sem=recv.at[BASE[name][1] + place], device_id=device, device_id_type=pl.DeviceIdType.MESH,
        )

    def arrived(ref, name, place=0):
        move(ref, ref, name, at_core, place).wait_recv()

    def left_here(ref, name):
        pending.append(move(ref, ref, name, at_core).wait_send)

    others = pl.ds(1, NX - 1)
    others_y = pl.ds(1, NY - 1)

    loads = []
    for i, (source, target) in enumerate(
        ((act_in, act), (basis_in, basis), (grads_in, grads), (first_in, first), (second_in, second))
    ):
        loads.append(pltpu.make_async_copy(source, target, load.at[i]))
    loads[0].start()
    loads[1].start()

    pending = []

    def finish():
        for wait in pending:
            wait()

    barrier = pltpu.get_barrier_semaphore()
    partners = [at_x(k) for k in range(1, NX)] + [at_y(k) for k in range(1, NY)] + [at_z(k) for k in range(1, NZ)]
    partners += [at_h, at_core]
    for device in partners:
        pl.semaphore_signal(barrier, inc=1, device_id=device, device_id_type=pl.DeviceIdType.MESH)

    holds = z == x
    owns = jnp.logical_and(holds, h == y // 2)

    loads[0].wait()
    loads[1].wait()

    def rows_h():
        return move(rows, rows, "rows_h", at_h)

    right, left = (z - x + NZ) % NZ, (x - z + NZ) % NZ

    def rows_z(way):
        return move(rows, rows, "rows_z", at_z(1 if way == 0 else NZ - 1), 0, way)

    def pass_rows(step):
        for way, hops in enumerate((right, left)):
            if step < NZ // 2 - way:

                @pl.when(hops == step)
                def _():
                    if step:
                        rows_z(0).wait_recv()
                    rows_z(way).start()

    def columns(k):
        return pl.ds(pl.multiple_of((z + k + x) % NX * CHUNK, CHUNK), CHUNK)

    def project(k):
        value = jnp.transpose(jnp.dot(act[...], basis[:, columns(k)], preferred_element_type=f32))
        value = value.reshape(NY, PARTS, ROWS, TOK)
        return [value[:, p].reshape(PART, TOK) for p in range(PARTS)]

    def reduce_z(p, k):
        return move(part_send.at[p, k], part_recv.at[p, k], "reduce_z", at_z(k), p)

    for i, k in enumerate(OFFSETS):
        for p, value in enumerate(project(k)):
            part_send[p, k] = value.astype(bf16)
        if i == 0:
            pl.semaphore_wait(barrier, len(partners))
        reduce_z(0, k).start()
    for p in range(1, PARTS):
        for k in OFFSETS:
            reduce_z(p, k).start()
    left_here(part_send.at[:, others], "reduce_z")
    for copy in loads[2:]:
        copy.start()

    @pl.when(owns)
    def _():
        rows[...] = basis[pl.ds(pl.multiple_of((y % 2 * 2 + c) * 128, 128), 128), :]
        rows_h().start()

    def sent_rows_h():
        @pl.when(owns)
        def _():
            rows_h().wait_send()

    pending.append(sent_rows_h)
    def pair_h(p):
        return move(half.at[p], half_recv.at[p], "pair_h", at_h, p)

    for p, value in enumerate(project(0)):
        own[p] = value
    for p in range(PARTS):
        total = own[p]
        arrived(part_recv.at[p, others], "reduce_z", p)
        for k in range(1, NZ):
            total = total + part_recv[p, k].astype(f32)
        half[p] = total
        pair_h(p).start()
    left_here(half, "pair_h")

    def gather_z(p, k):
        ranks = pl.ds(p * PART, PART)
        return move(turned.at[ranks], turned_recv.at[k, ranks], "gather_z", at_z(k), p * NZ + k)

    def relay_z(p):
        ranks = pl.ds(p * PART, PART)
        device = at_z(1 if RELAY[p] < NZ // 2 else NZ - 1)
        place = p * NZ + NZ // 2
        return move(turned_recv.at[RELAY[p], ranks], turned_recv.at[NZ // 2, ranks], "gather_z", device, place)

    def gather(p):
        pair_h(p).wait_recv()
        turned[pl.ds(p * PART, PART), :] = (half[p] + half_recv[p]).astype(bf16)
        gather_z(p, RELAY[p]).start()
        for k in GATHER[p]:
            if k not in (RELAY[p], NZ // 2):
                gather_z(p, k).start()

    def away(k):
        return (z - k + NZ) % NX

    def to_core(p, k):
        return move(full.at[k, p], core_recv.at[k], "pair_core", at_core, k)

    def to_x(o):
        return move(x_send.at[o], x_recv.at[o], "first_x", at_x(o))

    def to_y(q, o):
        return move(y_send.at[o, (y + q) % NY], y_recv.at[q, o], "first_y", at_y(q), o)

    def sum_cores(p, k):
        @pl.when(c == p)
        def _():
            to_core(p, k).wait_recv()
            o = away(k)
            both = full[k, p] + core_recv[k]
            mine[o] = both
            x_send[o] = both[:, :, :XF].astype(bf16)
            y_send[o] = both[:, :, XF:].astype(bf16)

            @pl.when(o != 0)
            def _():
                to_x(o).start()

            for q in SIDES:
                to_y(q, o).start()

    def gradient(p, k):
        if k:
            gather_z(p, k).wait_recv()
            if k == RELAY[p]:
                relay_z(p).start()
            block = turned_recv[k, pl.ds(p * PART, PART)]
        else:
            block = turned[pl.ds(p * PART, PART), :]
        product = jnp.dot(block, grads[...], preferred_element_type=f32)
        full[k, p] = product.reshape(NY, ROWS, FF)

        @pl.when(c != p)
        def _():
            to_core(p, k).start()

    loads[2].wait()
    work = [(p, k) for p in range(PARTS) for k in (0,) + GATHER[p]]
    gather(0)
    for i, (p, k) in enumerate(work):
        gradient(p, k)
        if i % NZ == 0 and p + 1 < PARTS:
            gather(p + 1)
        if i >= BEHIND:
            sum_cores(*work[i - BEHIND])
    for item in work[len(work) - BEHIND :]:
        sum_cores(*item)
    left_here(turned_recv.at[others], "gather_z")
    left_here(core_recv, "pair_core")
    left_here(x_send.at[others], "first_x")
    left_here(y_recv.at[others_y], "first_y")

    @pl.when(jnp.logical_and(holds, jnp.logical_not(owns)))
    def _():
        rows_h().wait_recv()

    pass_rows(0)

    def sent_rows_z():
        for way, hops in enumerate((right, left)):

            @pl.when(hops < NZ // 2 - way)
            def _():
                rows_z(way).wait_send()

    pending.append(sent_rows_z)

    def second_x(o):
        return move(u_send.at[o], u_recv.at[o], "second_x", at_x(o))

    def sum_y(o):
        value = mine[o, y][:, XF:]
        for q in range(1, NY):
            value = value + y_recv[q, o].astype(f32)
        return value

    for k in (0,) + NEAR:
        o = away(k)
        arrived(y_recv.at[others_y, o], "first_y", o)
        u_send[o] = sum_y(o).astype(bf16)

        @pl.when(o != 0)
        def _():
            second_x(o).start()

    left_here(u_send.at[others], "second_x")
    arrived(x_recv.at[others], "first_x")
    value = mine[0][:, :, :XF]
    for o in range(1, NX):
        value = value + x_recv[o].astype(f32)
    t_send[...] = value
    for q in SIDES:
        move(t_send.at[(y + q) % NY], t_recv.at[q], "second_y", at_y(q)).start()
    left_here(t_recv.at[others_y], "second_y")

    pass_rows(1)
    loads[3].wait()
    loads[4].wait()

    def adam(gradient, columns, target):
        new_first = beta_first * first[:, columns] + (1.0 - beta_first) * gradient
        new_second = beta_second * second[:, columns] + (1.0 - beta_second) * gradient * gradient
        first_hat = new_first / (1.0 - beta_first**STEP)
        second_hat = new_second / (1.0 - beta_second**STEP)
        first_out[:, columns] = new_first
        second_out[:, columns] = new_second
        target[x, y, c] = (first_hat / (jnp.sqrt(second_hat) + adam_eps)).astype(bf16)

    def x_from(o):
        return (x + NX - o) % NX

    def y_from(q):
        return (y + NY - q) % NY

    def x_one(o):
        ref = dir_one.at[x, y, c]
        return move(ref, ref, "x_one", at_x(o), o)

    def y_one(q, o):
        ref = dir_one.at[x_from(o), y, c]
        return move(ref, ref, "y_one", at_y(q), o)

    def y_two(q):
        ref = dir_two.at[x, y, c]
        return move(ref, ref, "y_two", at_y(q), q)

    def x_two(q, o):
        ref = dir_two.at[x, y_from(q), c]
        return move(ref, ref, "x_two", at_x(o), o)

    def share(array, name, o):
        ref = array.at[x_from(o), :, c]
        return move(ref, ref, name, at_core)

    arrived(t_recv.at[others_y], "second_y")
    value = t_send[y]
    for q in range(1, NY):
        value = value + t_recv[q]
    adam(value, slice(0, XF), dir_two)
    for q in SIDES:
        y_two(q).start()
    for o in OFFSETS:
        x_two(0, o).start()
    pass_rows(2)
    arrived(u_recv.at[others], "second_x")
    value = sum_y(0)
    for o in range(1, NX):
        value = value + u_recv[o].astype(f32)
    adam(value, slice(XF, FF), dir_one)
    for o in OFFSETS:
        x_one(o).start()
    for q in SIDES:
        y_one(q, 0).start()
    pass_rows(3)
    for q in SIDES:
        y_two(q).wait_recv()
        for o in OFFSETS:
            x_two(q, o).start()
    share(dir_two, "core_two", 0).start()
    for o in NEAR:
        x_one(o).wait_recv()
        for q in SIDES:
            y_one(q, o).start()
    for o in NEAR:
        arrived(dir_two.at[x_from(o), :, c], "x_two", o)
        share(dir_two, "core_two", o).start()
    for o in (0,) + NEAR:
        arrived(dir_one.at[x_from(o), pl.ds(0, NY - 1), c], "y_one", o)
        share(dir_one, "core_one", o).start()
    left_here(dir_one.at[others, 0, c], "x_one")
    left_here(dir_one.at[:, pl.ds(0, NY - 1), c], "y_one")
    left_here(dir_two.at[0, pl.ds(0, NY - 1), c], "y_two")
    left_here(dir_two.at[others, :, c], "x_two")
    left_here(dir_one.at[:, :, c], "core_one")
    left_here(dir_two.at[:, :, c], "core_two")

    @pl.when(jnp.logical_or(right == NZ // 2, left == NZ // 2 - 1))
    def _():
        rows_z(0).wait_recv()

    arrived(dir_two.at[:, :, 1 - c], "core_two")
    step_out[:, :XF] = galore_scale * jnp.dot(
        rows[...], dir_two[...].reshape(RANK, XF), preferred_element_type=f32
    )
    arrived(dir_one.at[:, :, 1 - c], "core_one")
    step_out[:, XF:] = galore_scale * jnp.dot(
        rows[...], dir_one[...].reshape(RANK, YF), preferred_element_type=f32
    )
    finish()


def body(activations, out_grads, basis, first_moment, second_moment):
    vmem = pl.BlockSpec(memory_space=pltpu.VMEM)
    return pl.pallas_call(
        kernel,
        out_shape=(
            jax.ShapeDtypeStruct((128, FF), f32),
            jax.ShapeDtypeStruct((ROWS, FF), f32),
            jax.ShapeDtypeStruct((ROWS, FF), f32),
        ),
        in_specs=[pl.BlockSpec(memory_space=pl.ANY)] * 5,
        out_specs=(vmem,) * 3,
        scratch_shapes=[
            pltpu.VMEM((TOK, 512), bf16),
            pltpu.VMEM((TOK, FF), bf16),
            pltpu.VMEM((512, RANK), bf16),
            pltpu.VMEM((ROWS, FF), f32),
            pltpu.VMEM((ROWS, FF), f32),
            pltpu.VMEM((PARTS, PART, TOK), f32),
            pltpu.VMEM((PARTS, NZ, PART, TOK), bf16),
            pltpu.VMEM((PARTS, NZ, PART, TOK), bf16),
            pltpu.VMEM((PARTS, PART, TOK), f32),
            pltpu.VMEM((PARTS, PART, TOK), f32),
            pltpu.VMEM((CHUNK, TOK), bf16),
            pltpu.VMEM((NZ, CHUNK, TOK), bf16),
            pltpu.VMEM((NX, PARTS, NY, ROWS, FF), f32),
            pltpu.VMEM((NX, NY, ROWS, FF), f32),
            pltpu.VMEM((NX, NY, ROWS, FF), f32),
            pltpu.VMEM((NX, NY, ROWS, XF), bf16),
            pltpu.VMEM((NX, NY, ROWS, XF), bf16),
            pltpu.VMEM((NX, NY, ROWS, YF), bf16),
            pltpu.VMEM((NY, NX, ROWS, YF), bf16),
            pltpu.VMEM((NY, ROWS, XF), f32),
            pltpu.VMEM((NY, ROWS, XF), f32),
            pltpu.VMEM((NX, ROWS, YF), bf16),
            pltpu.VMEM((NX, ROWS, YF), bf16),
            pltpu.VMEM((NX, NY, 2, ROWS, YF), bf16),
            pltpu.VMEM((NX, NY, 2, ROWS, XF), bf16),
            pltpu.VMEM((128, RANK), bf16),
            pltpu.SemaphoreType.DMA((SENDS,)),
            pltpu.SemaphoreType.DMA((RECVS,)),
            pltpu.SemaphoreType.DMA((5,)),
        ],
        compiler_params=pltpu.CompilerParams(
            collective_id=0, has_side_effects=True, vmem_limit_bytes=60 << 20
        ),
        cost_estimate=pl.CostEstimate(flops=10**9, bytes_accessed=4 << 20, transcendentals=0),
        name="galore_step",
    )(activations, out_grads, basis, first_moment, second_moment)


def solution(mesh):
    return jax.shard_map(
        body,
        mesh=mesh,
        in_specs=(P("dp", "mp"), P("dp", "mp"), P("mp", None), P("dp", "mp"), P("dp", "mp")),
        out_specs=(P("dp", "mp"), P("dp", "mp"), P("dp", "mp")),
        check_vma=False,
    )
```

```python
import jax
import jax.numpy as jnp
from jax import lax
from jax.experimental import pallas as pl
from jax.experimental.pallas import tpu as pltpu
from jax.sharding import PartitionSpec as P

STEP = 10

beta_first = 0.9
beta_second = 0.95
adam_eps = 1e-08
galore_scale = 0.25

NX, NY, NZ = 8, 4, 8
RANK = 1024
TOK = 256
FF = 896
CHUNK = RANK // NX
PARTS = 2
PART = CHUNK // PARTS
BEHIND = 3
ROWS = 16
XF = 384
YF = FF - XF
OFFSETS = (4, 3, 5, 2, 6, 1, 7)
NEAR = (1, 7, 2, 6, 3, 5, 4)
SIDES = (1, 3, 2)

f32, bf16 = jnp.float32, jnp.bfloat16

EXCHANGES = {
    "reduce_z": (1, PARTS), "pair_h": (1, PARTS), "gather_z": (1, PARTS * NZ), "pair_core": (1, NX),
    "first_x": (1, 1), "first_y": (1, NX), "second_y": (1, 1), "second_x": (1, 1),
    "x_one": (1, NX), "y_one": (1, NX), "y_two": (1, NY), "x_two": (1, NX), "core_one": (1, 1), "core_two": (1, 1),
    "rows_h": (1, 1), "rows_z": (2, 1),
}
SENDS, RECVS, BASE = 0, 0, {}
for name, (sends, recvs) in EXCHANGES.items():
    BASE[name] = (SENDS, RECVS)
    SENDS, RECVS = SENDS + sends, RECVS + recvs


def kernel(
    act_in, grads_in, basis_in, first_in, second_in, step_out, first_out, second_out,
    act, grads, basis, first, second,
    own, part_send, part_recv, half, half_recv, turned, turned_recv, full, core_recv, mine, x_send, x_recv,
    y_send, y_recv, t_send, t_recv, u_send, u_recv, dir_one, dir_two, rows, send, recv, load,
):
    dp, mp = lax.axis_index("dp"), lax.axis_index("mp")
    x, y, c = dp // (2 * NY), dp // 2 % NY, dp % 2
    z, h = mp // 2, mp % 2

    def at_x(k):
        return (((x + k) % NX * NY + y) * 2 + c, mp)

    def at_y(k):
        return ((x * NY + (y + k) % NY) * 2 + c, mp)

    def at_z(k):
        return (dp, (z + k) % NZ * 2 + h)

    at_h = (dp, z * 2 + 1 - h)
    at_core = (dp + 1 - 2 * c, mp)

    def move(source, target, name, device, place=0, send_place=0):
        return pltpu.make_async_remote_copy(
            src_ref=source, dst_ref=target, send_sem=send.at[BASE[name][0] + send_place],
            recv_sem=recv.at[BASE[name][1] + place], device_id=device, device_id_type=pl.DeviceIdType.MESH,
        )

    def arrived(ref, name, place=0):
        move(ref, ref, name, at_core, place).wait_recv()

    def left_here(ref, name):
        pending.append(move(ref, ref, name, at_core).wait_send)

    others = pl.ds(1, NX - 1)
    others_y = pl.ds(1, NY - 1)

    loads = []
    for i, (source, target) in enumerate(
        ((act_in, act), (basis_in, basis), (grads_in, grads), (first_in, first), (second_in, second))
    ):
        loads.append(pltpu.make_async_copy(source, target, load.at[i]))
    loads[0].start()
    loads[1].start()

    pending = []

    def finish():
        for wait in pending:
            wait()

    barrier = pltpu.get_barrier_semaphore()
    partners = [at_x(k) for k in range(1, NX)] + [at_y(k) for k in range(1, NY)] + [at_z(k) for k in range(1, NZ)]
    partners += [at_h, at_core]
    for device in partners:
        pl.semaphore_signal(barrier, inc=1, device_id=device, device_id_type=pl.DeviceIdType.MESH)

    holds = z == x
    owns = jnp.logical_and(holds, h == y // 2)

    loads[0].wait()
    loads[1].wait()

    @pl.when(owns)
    def _():
        rows[...] = basis[pl.ds(pl.multiple_of((y % 2 * 2 + c) * 128, 128), 128), :]

    def rows_h():
        return move(rows, rows, "rows_h", at_h)

    right, left = (z - x + NZ) % NZ, (x - z + NZ) % NZ

    def rows_z(way):
        return move(rows, rows, "rows_z", at_z(1 if way == 0 else NZ - 1), 0, way)

    def pass_rows(step):
        for way, hops in enumerate((right, left)):
            if step < NZ // 2 - way:

                @pl.when(hops == step)
                def _():
                    if step:
                        rows_z(0).wait_recv()
                    rows_z(way).start()

    def columns(k):
        return pl.ds(pl.multiple_of((z + k + x) % NX * CHUNK, CHUNK), CHUNK)

    def project(k):
        value = jnp.transpose(jnp.dot(act[...], basis[:, columns(k)], preferred_element_type=f32))
        value = value.reshape(NY, PARTS, ROWS, TOK)
        return [value[:, p].reshape(PART, TOK) for p in range(PARTS)]

    def reduce_z(p, k):
        return move(part_send.at[p, k], part_recv.at[p, k], "reduce_z", at_z(k), p)

    for i, k in enumerate(OFFSETS):
        for p, value in enumerate(project(k)):
            part_send[p, k] = value.astype(bf16)
        if i == 0:
            pl.semaphore_wait(barrier, len(partners))
        reduce_z(0, k).start()
    for p in range(1, PARTS):
        for k in OFFSETS:
            reduce_z(p, k).start()
    left_here(part_send.at[:, others], "reduce_z")
    for copy in loads[2:]:
        copy.start()

    @pl.when(owns)
    def _():
        rows_h().start()

    def sent_rows_h():
        @pl.when(owns)
        def _():
            rows_h().wait_send()

    pending.append(sent_rows_h)
    def pair_h(p):
        return move(half.at[p], half_recv.at[p], "pair_h", at_h, p)

    for p, value in enumerate(project(0)):
        own[p] = value
    for p in range(PARTS):
        total = own[p]
        arrived(part_recv.at[p, others], "reduce_z", p)
        for k in range(1, NZ):
            total = total + part_recv[p, k].astype(f32)
        own[p] = total
        half[p] = total.astype(bf16)
        pair_h(p).start()
    left_here(half, "pair_h")

    def gather_z(p, k):
        ranks = pl.ds(p * PART, PART)
        return move(turned.at[ranks], turned_recv.at[k, ranks], "gather_z", at_z(k), p * NZ + k)

    def gather(p):
        pair_h(p).wait_recv()
        turned[pl.ds(p * PART, PART), :] = (own[p] + half_recv[p].astype(f32)).astype(bf16)
        for k in NEAR:
            gather_z(p, k).start()

    def away(k):
        return (z - k + NZ) % NX

    def to_core(p, k):
        return move(full.at[k, p], core_recv.at[k], "pair_core", at_core, k)

    def to_x(o):
        return move(x_send.at[o], x_recv.at[o], "first_x", at_x(o))

    def to_y(q, o):
        return move(y_send.at[o, (y + q) % NY], y_recv.at[q, o], "first_y", at_y(q), o)

    def sum_cores(p, k):
        @pl.when(c == p)
        def _():
            to_core(p, k).wait_recv()
            o = away(k)
            both = full[k, p] + core_recv[k]
            mine[o] = both
            x_send[o] = both[:, :, :XF].astype(bf16)
            y_send[o] = both[:, :, XF:].astype(bf16)

            @pl.when(o != 0)
            def _():
                to_x(o).start()

            for q in SIDES:
                to_y(q, o).start()

    def gradient(p, k):
        if k:
            gather_z(p, k).wait_recv()
            block = turned_recv[k, pl.ds(p * PART, PART)]
        else:
            block = turned[pl.ds(p * PART, PART), :]
        product = jnp.dot(block, grads[...], preferred_element_type=f32)
        full[k, p] = product.reshape(NY, ROWS, FF)

        @pl.when(c != p)
        def _():
            to_core(p, k).start()

    loads[2].wait()
    work = [(p, k) for p in range(PARTS) for k in (0,) + NEAR]
    gather(0)
    for i, (p, k) in enumerate(work):
        gradient(p, k)
        if i % NZ == 0 and p + 1 < PARTS:
            gather(p + 1)
        if i >= BEHIND:
            sum_cores(*work[i - BEHIND])
    for item in work[len(work) - BEHIND :]:
        sum_cores(*item)
    left_here(turned_recv.at[others], "gather_z")
    left_here(core_recv, "pair_core")
    left_here(x_send.at[others], "first_x")
    left_here(y_recv.at[others_y], "first_y")

    @pl.when(jnp.logical_and(holds, jnp.logical_not(owns)))
    def _():
        rows_h().wait_recv()

    pass_rows(0)

    def sent_rows_z():
        for way, hops in enumerate((right, left)):

            @pl.when(hops < NZ // 2 - way)
            def _():
                rows_z(way).wait_send()

    pending.append(sent_rows_z)

    def second_x(o):
        return move(u_send.at[o], u_recv.at[o], "second_x", at_x(o))

    def sum_y(o):
        value = mine[o, y][:, XF:]
        for q in range(1, NY):
            value = value + y_recv[q, o].astype(f32)
        return value

    for k in (0,) + NEAR:
        o = away(k)
        arrived(y_recv.at[others_y, o], "first_y", o)
        u_send[o] = sum_y(o).astype(bf16)

        @pl.when(o != 0)
        def _():
            second_x(o).start()

    left_here(u_send.at[others], "second_x")
    arrived(x_recv.at[others], "first_x")
    value = mine[0][:, :, :XF]
    for o in range(1, NX):
        value = value + x_recv[o].astype(f32)
    t_send[...] = value
    for q in SIDES:
        move(t_send.at[(y + q) % NY], t_recv.at[q], "second_y", at_y(q)).start()
    left_here(t_recv.at[others_y], "second_y")

    pass_rows(1)
    loads[3].wait()
    loads[4].wait()

    def adam(gradient, columns, target):
        new_first = beta_first * first[:, columns] + (1.0 - beta_first) * gradient
        new_second = beta_second * second[:, columns] + (1.0 - beta_second) * gradient * gradient
        first_hat = new_first / (1.0 - beta_first**STEP)
        second_hat = new_second / (1.0 - beta_second**STEP)
        first_out[:, columns] = new_first
        second_out[:, columns] = new_second
        target[x, y, c] = (first_hat / (jnp.sqrt(second_hat) + adam_eps)).astype(bf16)

    def x_from(o):
        return (x + NX - o) % NX

    def y_from(q):
        return (y + NY - q) % NY

    def x_one(o):
        ref = dir_one.at[x, y, c]
        return move(ref, ref, "x_one", at_x(o), o)

    def y_one(q, o):
        ref = dir_one.at[x_from(o), y, c]
        return move(ref, ref, "y_one", at_y(q), o)

    def y_two(q):
        ref = dir_two.at[x, y, c]
        return move(ref, ref, "y_two", at_y(q), q)

    def x_two(q, o):
        ref = dir_two.at[x, y_from(q), c]
        return move(ref, ref, "x_two", at_x(o), o)

    def share(array, name, o):
        ref = array.at[x_from(o), :, c]
        return move(ref, ref, name, at_core)

    arrived(t_recv.at[others_y], "second_y")
    value = t_send[y]
    for q in range(1, NY):
        value = value + t_recv[q]
    adam(value, slice(0, XF), dir_two)
    for q in SIDES:
        y_two(q).start()
    for o in OFFSETS:
        x_two(0, o).start()
    pass_rows(2)
    arrived(u_recv.at[others], "second_x")
    value = sum_y(0)
    for o in range(1, NX):
        value = value + u_recv[o].astype(f32)
    adam(value, slice(XF, FF), dir_one)
    for o in OFFSETS:
        x_one(o).start()
    for q in SIDES:
        y_one(q, 0).start()
    pass_rows(3)
    for q in SIDES:
        y_two(q).wait_recv()
        for o in OFFSETS:
            x_two(q, o).start()
    share(dir_two, "core_two", 0).start()
    for o in NEAR:
        x_one(o).wait_recv()
        for q in SIDES:
            y_one(q, o).start()
    for o in NEAR:
        arrived(dir_two.at[x_from(o), :, c], "x_two", o)
        share(dir_two, "core_two", o).start()
    for o in (0,) + NEAR:
        arrived(dir_one.at[x_from(o), pl.ds(0, NY - 1), c], "y_one", o)
        share(dir_one, "core_one", o).start()
    left_here(dir_one.at[others, 0, c], "x_one")
    left_here(dir_one.at[:, pl.ds(0, NY - 1), c], "y_one")
    left_here(dir_two.at[0, pl.ds(0, NY - 1), c], "y_two")
    left_here(dir_two.at[others, :, c], "x_two")
    left_here(dir_one.at[:, :, c], "core_one")
    left_here(dir_two.at[:, :, c], "core_two")

    @pl.when(jnp.logical_or(right == NZ // 2, left == NZ // 2 - 1))
    def _():
        rows_z(0).wait_recv()

    arrived(dir_two.at[:, :, 1 - c], "core_two")
    step_out[:, :XF] = galore_scale * jnp.dot(
        rows[...], dir_two[...].reshape(RANK, XF), preferred_element_type=f32
    )
    arrived(dir_one.at[:, :, 1 - c], "core_one")
    step_out[:, XF:] = galore_scale * jnp.dot(
        rows[...], dir_one[...].reshape(RANK, YF), preferred_element_type=f32
    )
    finish()


def body(activations, out_grads, basis, first_moment, second_moment):
    vmem = pl.BlockSpec(memory_space=pltpu.VMEM)
    return pl.pallas_call(
        kernel,
        out_shape=(
            jax.ShapeDtypeStruct((128, FF), f32),
            jax.ShapeDtypeStruct((ROWS, FF), f32),
            jax.ShapeDtypeStruct((ROWS, FF), f32),
        ),
        in_specs=[pl.BlockSpec(memory_space=pl.ANY)] * 5,
        out_specs=(vmem,) * 3,
        scratch_shapes=[
            pltpu.VMEM((TOK, 512), bf16),
            pltpu.VMEM((TOK, FF), bf16),
            pltpu.VMEM((512, RANK), bf16),
            pltpu.VMEM((ROWS, FF), f32),
            pltpu.VMEM((ROWS, FF), f32),
            pltpu.VMEM((PARTS, PART, TOK), f32),
            pltpu.VMEM((PARTS, NZ, PART, TOK), bf16),
            pltpu.VMEM((PARTS, NZ, PART, TOK), bf16),
            pltpu.VMEM((PARTS, PART, TOK), bf16),
            pltpu.VMEM((PARTS, PART, TOK), bf16),
            pltpu.VMEM((CHUNK, TOK), bf16),
            pltpu.VMEM((NZ, CHUNK, TOK), bf16),
            pltpu.VMEM((NX, PARTS, NY, ROWS, FF), f32),
            pltpu.VMEM((NX, NY, ROWS, FF), f32),
            pltpu.VMEM((NX, NY, ROWS, FF), f32),
            pltpu.VMEM((NX, NY, ROWS, XF), bf16),
            pltpu.VMEM((NX, NY, ROWS, XF), bf16),
            pltpu.VMEM((NX, NY, ROWS, YF), bf16),
            pltpu.VMEM((NY, NX, ROWS, YF), bf16),
            pltpu.VMEM((NY, ROWS, XF), f32),
            pltpu.VMEM((NY, ROWS, XF), f32),
            pltpu.VMEM((NX, ROWS, YF), bf16),
            pltpu.VMEM((NX, ROWS, YF), bf16),
            pltpu.VMEM((NX, NY, 2, ROWS, YF), bf16),
            pltpu.VMEM((NX, NY, 2, ROWS, XF), bf16),
            pltpu.VMEM((128, RANK), bf16),
            pltpu.SemaphoreType.DMA((SENDS,)),
            pltpu.SemaphoreType.DMA((RECVS,)),
            pltpu.SemaphoreType.DMA((5,)),
        ],
        compiler_params=pltpu.CompilerParams(
            collective_id=0, has_side_effects=True, vmem_limit_bytes=60 << 20
        ),
        cost_estimate=pl.CostEstimate(flops=10**9, bytes_accessed=4 << 20, transcendentals=0),
        name="galore_step",
    )(activations, out_grads, basis, first_moment, second_moment)


def solution(mesh):
    return jax.shard_map(
        body,
        mesh=mesh,
        in_specs=(P("dp", "mp"), P("dp", "mp"), P("mp", None), P("dp", "mp"), P("dp", "mp")),
        out_specs=(P("dp", "mp"), P("dp", "mp"), P("dp", "mp")),
        check_vma=False,
    )
```
